32 devices in a mesh: expert: 4 (over y, core), tensor: 8 (over z, x).
Axes of the slice: x: 2, y: 2, z: 4, core: 2. Of those that a mesh axis runs over, the one named last changes fastest.
Arguments:
- tokens: bfloat16 [1024, 6144], P('expert', 'tensor'), may hold values from -6 to 6
- expert_ids: int32 [1024, 2], P('expert'), may hold values from 0 to 3, all different within a row; in each aligned block of 256 rows (0 to 255, 256 to 511, ...) at most 192 rows name the same one
- gate_prob: float32 [1024, 2], P('expert'), may hold values from 0.1 to 1
- w_gate: bfloat16 [4, 6144, 8192], P('expert', None, 'tensor'), may hold values from -0.078125 to 0.078125
- w_up: bfloat16 [4, 6144, 8192], P('expert', None, 'tensor'), may hold values from -0.078125 to 0.078125
- w_down: bfloat16 [4, 8192, 6144], P('expert', 'tensor'), may hold values from -0.09375 to 0.09375
Outputs:
- mixed: bfloat16 [1024, 6144], P('expert', 'tensor')
The draws below stay inside these ranges and needn't reach their ends.
Inputs may be any that keep to these rules, and one draw needn't show every extreme that they name: `expert_ids`: the two experts of a row differ. Within the rows of one index of expert (aligned blocks of 256 rows) no expert is named by more than 192 rows, and in every draw some expert is named by exactly 192 rows of some block.
All inputs are finite; a program needn't handle non-finite values.
Results may differ from the reference program's by a relative error of at most 0.017.
Values may be sent and summed in bfloat16 or wider, within the bound.
A program may use at most 128 MiB of HBM per device.

```python
import math
import jax
import jax.numpy as jnp
import numpy as np
from jax import lax

D = 6144
FF = 8192
TOK_G = 256
EXPERTS = 4
CAP = 192
TOKENS = 1024
N_EXPERT = 4
N_TENSOR = 8


def with_spikes(entries, rng, source, target, shards_of, factor):
    owner, partner = [(jnp.arange(entries.shape[dim]) // (entries.shape[dim] // shards_of)).reshape([-1 if axis == dim else 1 for axis in range(entries.ndim)]) for dim in (source, target)]
    chosen = jax.random.permutation(rng, shards_of)[partner]
    strong = (owner == chosen) | (owner == (partner + shards_of // 2) % shards_of)
    return jnp.where(strong, factor * entries, entries)


def block_scale(key, dims, shards, low, largest):
    loudness = 1.0
    for dim, shards_of in shards:
        heights = jax.random.uniform(jax.random.fold_in(jax.random.fold_in(key, 6), dim), (shards_of,), jnp.float32, low / len(shards), largest / len(shards))
        loudness = loudness * jnp.repeat(jnp.exp(heights), dims[dim] // shards_of).reshape((-1,) + (1,) * (len(dims) - 1 - dim))
    return loudness


def shared_out(stream_key, own, number, rows, number_of, top, bound, skew):
    ranking = jax.random.permutation(stream_key, number_of)
    heavy_load, ordinary = shares(number_of, rows * top, bound, skew, True), shares(number_of, rows * top, bound, skew, False)
    places = jnp.arange(number_of)

    def named(sizes, rotation):
        used = int((sizes > 0).sum())
        fixed = max(1, used // 4)
        moved = fixed + (places - fixed + rotation * (used - fixed)) % max(1, number_of - fixed)
        return jnp.zeros((number_of,), jnp.int32).at[ranking[jnp.where(places < fixed, places, moved)]].set(jnp.asarray(sizes, jnp.int32))

    sizes = jnp.where(number % 4 == 0, named(heavy_load, number // 4), named(ordinary, number - number // 4 - 1))
    mixed = jax.random.permutation(jax.random.fold_in(own, 3), number_of)
    donor, sink = mixed[0:number_of // 2 * 2:2], mixed[1:number_of // 2 * 2:2]
    room = jnp.minimum(sizes[donor] - 1, bound - sizes[sink]) // 2
    room = jnp.where((donor == ranking[0]) | (sink == ranking[0]) | (sizes[sink] == 0), 0, jnp.maximum(room, 0))
    moved = jax.random.randint(jax.random.fold_in(own, 4), (number_of // 2,), 0, 1 << 20) % (room + 1)
    sizes = sizes.at[donor].add(-moved).at[sink].add(moved)
    members = jnp.searchsorted(jnp.cumsum(sizes), jnp.arange(rows * top), side="right").astype(jnp.int32)
    table = members.reshape(top, rows).T
    table = table[jax.random.permutation(jax.random.fold_in(own, 1), rows)]
    rotation = jax.random.randint(jax.random.fold_in(own, 2), (rows, 1), 0, top)
    return jnp.take_along_axis(table, (jnp.arange(top)[None, :] + rotation) % top, axis=1)


def shares(count, total, most, skew, full):
    weights = [(1 << 20) // math.isqrt(rank ** skew) + 1 for rank in range(1, count + 1)]
    largest = most if full else min(most, max(-(-total // count), total * weights[0] // sum(weights)))
    least = 1 if total - largest >= count - 1 else 0
    given, spare = [largest] + [least] * (count - 1), total - largest - least * (count - 1)
    while spare > 0:
        candidates = [i for i in range(1, count) if given[i] < largest] or [i for i in range(1, count) if given[i] < most]
        mass, budget = sum([weights[i] for i in candidates]), spare
        for i in candidates:
            more = min(most - given[i], max(1, budget * weights[i] // mass), spare)
            given[i] = given[i] + more
            spare = spare - more
    return np.array(given)


def normal_values(stream_key, dims, deviation, bound, split=(), kind=jnp.bfloat16):
    values = jax.random.normal(stream_key, dims, jnp.float32) * deviation
    if len(split) > 0:
        values = block_scale(stream_key, dims, split, -0.22, 0.18) * values
    return jnp.clip(values, min=-bound, max=bound).astype(kind)


def noise_with(own_key, dims, scale, bound, shards, heavy, kind=jnp.bfloat16):
    result = scale * jax.random.normal(own_key, dims, jnp.float32)
    if shards:
        result = result * block_scale(own_key, dims, shards, -0.22, 0.18)
    return jnp.clip(with_spikes(result, jax.random.fold_in(own_key, 3), *heavy), -bound, bound).astype(kind)


def setup_inputs(seed: int = 0) -> dict:
    streams_of = jax.random.split(jax.random.key(seed), 7)
    tokens = normal_values(streams_of[0], (TOKENS, D), 1.0, 6.0, ((0, 4), (1, 8)))
    expert_ids_keys = jax.random.split(jax.random.fold_in(streams_of[1], 1), TOKENS // TOK_G)
    expert_ids_turns = jax.random.permutation(jax.random.fold_in(streams_of[1], 3), TOKENS // TOK_G)
    expert_ids = jax.vmap(lambda own, number: shared_out(jax.random.fold_in(streams_of[1], 2), own, number, TOK_G, EXPERTS, 2, CAP, 2))(expert_ids_keys, expert_ids_turns).reshape((TOKENS, 2))
    gate_prob = jnp.clip(0.1 + 0.9 * jax.random.uniform(streams_of[2], (TOKENS, 2), jnp.float32) ** block_scale(streams_of[2], (TOKENS, 2), ((0, 4),), -0.2, 0.2), 0.1, 1.0)
    w_gate = normal_values(streams_of[3], (EXPERTS, D, FF), D ** -0.5, 0.078125, ((0, 4), (2, 8)))
    w_up = normal_values(streams_of[4], (EXPERTS, D, FF), D ** -0.5, 0.078125, ((0, 4), (2, 8)))
    w_down = noise_with(streams_of[5], (EXPERTS, FF, D), FF ** -0.5, 0.09375, ((0, 4), (1, 8)), (1, 2, 8, 2.0))
    return dict(tokens=tokens, expert_ids=expert_ids, gate_prob=gate_prob, w_gate=w_gate, w_up=w_up, w_down=w_down)


def slot_table(ids, experts, cap):
    flat = ids.reshape(-1)
    onehot = (flat[:, None] == jnp.arange(experts, dtype=jnp.int32)[None, :]).astype(jnp.int32)
    before = jnp.cumsum(onehot, axis=0) - onehot
    position = jnp.sum(before * onehot, axis=1)
    slot = flat * cap + position
    match = slot[None, :] == jnp.arange(experts * cap, dtype=jnp.int32)[:, None]
    which = jnp.arange(flat.shape[0], dtype=jnp.int32) // 2
    owner = jnp.max(jnp.where(match, which[None, :], -1), axis=1)
    return slot, owner


def reference(tokens, expert_ids, gate_prob, w_gate, w_up, w_down):
    group_rows = []
    group_slots = []
    for group in range(N_EXPERT):
        block = tokens[group * TOK_G:(group + 1) * TOK_G]
        slot, owner = slot_table(expert_ids[group * TOK_G:(group + 1) * TOK_G], EXPERTS, CAP)
        picked = jnp.take(block, jnp.maximum(owner, 0), axis=0)
        picked = jnp.where((owner >= 0)[:, None], picked, jnp.zeros_like(picked))
        group_rows.append(picked.reshape(EXPERTS, CAP, D))
        group_slots.append(slot)
    rows_all = jnp.stack(group_rows, axis=1)
    width = FF // N_TENSOR
    outs = []
    for expert in range(EXPERTS):
        rows = rows_all[expert].reshape(N_EXPERT * CAP, D)
        gate = jnp.dot(rows, w_gate[expert], preferred_element_type=jnp.float32)
        up = jnp.dot(rows, w_up[expert], preferred_element_type=jnp.float32)
        hidden = (jax.nn.silu(gate) * up).astype(jnp.bfloat16)
        down = w_down[expert]

        def add_block(index, total):
            start = (index * width).astype(jnp.int32)
            hid = lax.dynamic_slice_in_dim(hidden, start, width, 1)
            wts = lax.dynamic_slice_in_dim(down, start, width, 0)
            term = jnp.dot(hid, wts, preferred_element_type=jnp.float32)
            term = lax.optimization_barrier(term.astype(jnp.bfloat16)).astype(jnp.float32)
            return total + term

        total = lax.fori_loop(0, N_TENSOR, add_block, jnp.zeros((N_EXPERT * CAP, D), jnp.float32))
        outs.append(total.reshape(N_EXPERT, CAP, D))
    out_all = jnp.stack(outs, axis=0)
    results = []
    for group in range(N_EXPERT):
        table = out_all[:, group].reshape(EXPERTS * CAP, D)
        picked = jnp.take(table, group_slots[group], axis=0).reshape(TOK_G, 2, D)
        weights = gate_prob[group * TOK_G:(group + 1) * TOK_G]
        results.append(jnp.sum(weights[:, :, None] * picked, axis=1).astype(jnp.bfloat16))
    return jnp.concatenate(results, axis=0)
```

```python
import jax
import jax.numpy as jnp
from jax import lax
from jax.sharding import PartitionSpec as P


def local(tokens, expert_ids, gate_prob, w_gate, w_up, w_down):
    experts = lax.axis_size("expert")
    me = lax.axis_index("expert")
    chips = experts // 2
    rows = tokens.shape[0]
    swap = [(e, e ^ 1) for e in range(experts)]
    across = [[2 * y + c for y in range(chips)] for c in range(2)]

    def weights(ids, prob):
        return jnp.sum(jnp.where(ids == me, prob, 0.0), axis=1)

    ids_all = lax.all_gather(expert_ids, "expert", axis=0)
    prob_all = lax.all_gather(gate_prob, "expert", axis=0)
    core = lax.rem(me, 2)
    ids_pair = ids_all.reshape(chips, 2, rows, 2)
    prob_pair = prob_all.reshape(chips, 2, rows, 2)

    def of_core(c):
        ids = lax.dynamic_index_in_dim(ids_pair, c, 1, keepdims=False)
        prob = lax.dynamic_index_in_dim(prob_pair, c, 1, keepdims=False)
        return weights(ids.reshape(chips * rows, 2), prob.reshape(chips * rows, 2))

    column = lax.all_gather(tokens, "expert", axis=0, tiled=True, axis_index_groups=across)
    mine = lax.all_gather(column, "tensor", axis=1, tiled=True)
    theirs = lax.ppermute(mine, "expert", swap)

    def ffn(x, weight):
        gate = jnp.dot(x, w_gate[0], preferred_element_type=jnp.float32)
        up = jnp.dot(x, w_up[0], preferred_element_type=jnp.float32)
        hidden = (jax.nn.silu(gate) * up).astype(jnp.bfloat16)
        out = jnp.dot(hidden, w_down[0], preferred_element_type=jnp.float32)
        return out * weight[:, None]

    part_mine = ffn(mine, of_core(core))
    part_theirs = ffn(theirs, of_core(1 - core)).astype(jnp.bfloat16)
    arrived = lax.ppermute(part_theirs, "expert", swap)
    total = (part_mine + arrived.astype(jnp.float32)).astype(jnp.bfloat16)
    summed = lax.psum_scatter(total, "tensor", scatter_dimension=1, tiled=True)
    out = lax.psum_scatter(
        summed.astype(jnp.float32).astype(jnp.bfloat16),
        "expert",
        scatter_dimension=0,
        tiled=True,
        axis_index_groups=across,
    )
    return out.astype(jnp.bfloat16)


def solution(mesh):
    return jax.shard_map(
        local,
        mesh=mesh,
        in_specs=(
            P("expert", "tensor"),
            P("expert", None),
            P("expert", None),
            P("expert", None, "tensor"),
            P("expert", None, "tensor"),
            P("expert", "tensor", None),
        ),
        out_specs=P("expert", "tensor"),
        check_vma=False,
    )
```

```python
import functools

import jax
import jax.numpy as jnp
from jax import lax
from jax.experimental import pallas as pl
from jax.experimental.pallas import tpu as pltpu
from jax.sharding import PartitionSpec as P

MESH = pl.DeviceIdType.MESH
VMEM_LIMIT = 56 * 1024 * 1024


def place(nx, nz):
    e, t = lax.axis_index("expert"), lax.axis_index("tensor")
    y, core = e // 2, lax.rem(e, 2)
    z, x = t // nx, lax.rem(t, nx)
    return e, x, y, z, core


def greet(lines):
    barrier = pltpu.get_barrier_semaphore()
    for device in lines:
        pl.semaphore_signal(barrier, inc=1, device_id=device, device_id_type=MESH)
    pl.semaphore_wait(barrier, len(lines))


def remote(src, dst, sems, device):
    send, recv = sems
    return pltpu.make_async_remote_copy(
        src_ref=src,
        dst_ref=dst,
        send_sem=send,
        recv_sem=recv,
        device_id=device,
        device_id_type=MESH,
    )


def gather_kernel(
    nx, ny, nz, own_ref, aux_ref, g_ref, all_ref, s1, r1, s2, r2, s3, r3, sa, ra, local_sem
):
    e, x, y, z, core = place(nx, nz)
    experts = 2 * ny
    half = own_ref.shape[0] // 2
    t = z * nx + x

    def at_z(d):
        return (e, lax.rem(z + d, nz) * nx + x)

    def at_x(j):
        return (e, z * nx + lax.rem(x + j, nx))

    def at_y(j):
        return (lax.rem(y + j, ny) * 2 + core, t)

    def at_e(j):
        return (lax.rem(e + j, experts), t)

    greet(
        [at_z(d) for d in range(1, nz)]
        + [at_x(j) for j in range(1, nx)]
        + [at_e(j) for j in range(1, experts)]
    )
    waits = []
    rows = [pl.ds(0, half), pl.ds(half, half)]
    for h in range(2):
        keep = pltpu.make_async_copy(
            own_ref.at[rows[h]], g_ref.at[y, z, x, rows[h]], local_sem.at[h]
        )
        keep.start()
        waits.append((keep, False))
    first = {}
    for d in range(1, nz):
        for h in range(2):
            c = remote(
                own_ref.at[rows[h]],
                g_ref.at[y, z, x, rows[h]],
                (s1.at[h, d], r1.at[h, d]),
                at_z(d),
            )
            c.start()
            first[h, d] = c
    aux = []
    keep = pltpu.make_async_copy(aux_ref, all_ref.at[e], local_sem.at[2])
    keep.start()
    waits.append((keep, False))
    for j in range(1, experts):
        c = remote(aux_ref, all_ref.at[e], (sa.at[j], ra.at[j]), at_e(j))
        c.start()
        aux.append(c)

    second, third = {}, {}

    def forward(d):
        zs = lax.rem(z + nz - d, nz)
        for h in range(2):
            if d:
                first[h, d].wait_recv()
                src = g_ref.at[y, zs, x, rows[h]]
            else:
                src = own_ref.at[rows[h]]
            n, to = ((nx, at_x), (ny, at_y))[h]
            for j in range(1, n):
                c = remote(
                    src, g_ref.at[y, zs, x, rows[h]], (s2.at[h, d, j], r2.at[h, d, j]), to(j)
                )
                c.start()
                second[h, d, j] = c

    def spread(d):
        zs = lax.rem(z + nz - d, nz)
        for h in range(2):
            n, m, to = ((nx, ny, at_y), (ny, nx, at_x))[h]
            for j in range(1, n):
                second[h, d, j].wait_recv()
            if d == 0:
                waits[h][0].wait()
            slab = g_ref.at[y, zs, :, rows[h]] if h == 0 else g_ref.at[:, zs, x, rows[h]]
            for k in range(1, m):
                c = remote(slab, slab, (s3.at[h, d, k], r3.at[h, d, k]), to(k))
                c.start()
                third[h, d, k] = c

    forward(0)
    for d in range(1, nz):
        forward(d)
        spread(d - 1)
    spread(nz - 1)
    for c in third.values():
        c.wait_recv()
    for c in aux:
        c.wait()
    waits[2][0].wait()
    for c in [*first.values(), *second.values(), *third.values()]:
        c.wait_send()


def gather(tokens, aux, nx, ny, nz):
    rows, columns = tokens.shape
    n = max(nx, ny)
    dma = pltpu.SemaphoreType.DMA
    size = tokens.size * 2 * nx * ny * nz
    return pl.pallas_call(
        functools.partial(gather_kernel, nx, ny, nz),
        out_shape=(
            jax.ShapeDtypeStruct((ny, nz, nx, rows, columns), tokens.dtype),
            jax.ShapeDtypeStruct((2 * ny, *aux.shape), aux.dtype),
        ),
        in_specs=[pl.BlockSpec(memory_space=pl.ANY)] * 2,
        out_specs=[pl.BlockSpec(memory_space=pl.ANY)] * 2,
        scratch_shapes=[
            dma((2, nz)),
            dma((2, nz)),
            dma((2, nz, n)),
            dma((2, nz, n)),
            dma((2, nz, n)),
            dma((2, nz, n)),
            dma((2 * ny,)),
            dma((2 * ny,)),
            dma((3,)),
        ],
        cost_estimate=pl.CostEstimate(flops=0, bytes_accessed=2 * size, transcendentals=0),
        compiler_params=pltpu.CompilerParams(collective_id=0, has_side_effects=True),
    )(tokens, aux)


def reduce_kernel(
    nx, ny, nz, p_ref, o_ref, ya, xa, yb, xb, yc, xc, za, zb, s1, r1, s2, r2, s3, r3
):
    e, x, y, z, core = place(nx, nz)
    half = o_ref.shape[0] // 2
    t = z * nx + x
    f32 = jnp.float32

    def at_z(d):
        return (e, lax.rem(z + d, nz) * nx + x)

    def at_x(j):
        return (e, z * nx + lax.rem(x + j, nx))

    def at_y(j):
        return (lax.rem(y + j, ny) * 2 + core, t)

    greet(
        [at_z(d) for d in range(1, nz)]
        + [at_x(j) for j in range(1, nx)]
        + [at_y(j) for j in range(1, ny)]
    )
    rows = [pl.ds(0, half), pl.ds(half, half)]
    order = [*range(1, nz), 0]
    one, two, three = {}, {}, {}
    got, held, last = (ya, xa), (yb, xb), (yc, xc)
    for d in order:
        zt = lax.rem(z + d, nz)
        for h in range(2):
            n, to = ((ny, at_y), (nx, at_x))[h]
            for j in range(1, n):
                if h == 0:
                    src = p_ref.at[lax.rem(y + j, ny), zt, :, rows[h]]
                else:
                    src = p_ref.at[:, zt, lax.rem(x + j, nx), rows[h]]
                c = remote(src, got[h].at[d, j - 1], (s1.at[h, d, j], r1.at[h, d, j]), to(j))
                c.start()
                one[h, d, j] = c

    def middle(d):
        zt = lax.rem(z + d, nz)
        for h in range(2):
            n, m, to, at = ((ny, nx, at_x, x), (nx, ny, at_y, y))[h]
            for j in range(1, n):
                one[h, d, j].wait_recv()

            def add(i, _, h=h, n=n):
                if h == 0:
                    total = p_ref[y, zt, i, rows[h]].astype(f32)
                else:
                    total = p_ref[i, zt, x, rows[h]].astype(f32)
                for j in range(n - 1):
                    total += got[h][d, j, i].astype(f32)
                held[h][d, i] = total.astype(held[h].dtype)
                return 0

            lax.fori_loop(0, m, add, 0)
            for k in range(1, m):
                c = remote(
                    held[h].at[d, lax.rem(at + k, m)],
                    last[h].at[d, k - 1],
                    (s2.at[h, d, k], r2.at[h, d, k]),
                    to(k),
                )
                c.start()
                two[h, d, k] = c

    def end(d):
        for h in range(2):
            m, at = ((nx, x), (ny, y))[h]
            for k in range(1, m):
                two[h, d, k].wait_recv()
            total = held[h][d, at].astype(f32)
            for k in range(m - 1):
                total += last[h][d, k].astype(f32)
            za[h, d] = total.astype(za.dtype)
            if d:
                c = remote(za.at[h, d], zb.at[h, d - 1], (s3.at[h, d], r3.at[h, d]), at_z(d))
                c.start()
                three[h, d] = c

    for i, d in enumerate(order):
        middle(d)
        if i:
            end(order[i - 1])
    end(order[-1])
    for h in range(2):
        total = za[h, 0].astype(f32)
        for d in range(1, nz):
            three[h, d].wait_recv()
            total += zb[h, d - 1].astype(f32)
        o_ref[rows[h], :] = total.astype(o_ref.dtype)
    for c in [*one.values(), *two.values(), *three.values()]:
        c.wait_send()


def reduce_parts(parts, nx, ny, nz):
    rows, columns = parts.shape[-2:]
    half, n = rows // 2, max(nx, ny)
    kind = parts.dtype
    dma = pltpu.SemaphoreType.DMA
    return pl.pallas_call(
        functools.partial(reduce_kernel, nx, ny, nz),
        out_shape=jax.ShapeDtypeStruct((rows, columns), kind),
        in_specs=[pl.BlockSpec(memory_space=pltpu.VMEM)],
        out_specs=pl.BlockSpec(memory_space=pltpu.VMEM),
        scratch_shapes=[
            pltpu.VMEM((nz, ny - 1, nx, half, columns), kind),
            pltpu.VMEM((nz, nx - 1, ny, half, columns), kind),
            pltpu.VMEM((nz, nx, half, columns), kind),
            pltpu.VMEM((nz, ny, half, columns), kind),
            pltpu.VMEM((nz, nx - 1, half, columns), kind),
            pltpu.VMEM((nz, ny - 1, half, columns), kind),
            pltpu.VMEM((2, nz, half, columns), kind),
            pltpu.VMEM((2, nz - 1, half, columns), kind),
            dma((2, nz, n)),
            dma((2, nz, n)),
            dma((2, nz, n)),
            dma((2, nz, n)),
            dma((2, nz)),
            dma((2, nz)),
        ],
        cost_estimate=pl.CostEstimate(flops=0, bytes_accessed=4 * parts.size, transcendentals=0),
        compiler_params=pltpu.CompilerParams(
            collective_id=1, has_side_effects=True, vmem_limit_bytes=VMEM_LIMIT
        ),
    )(parts)


def local(tokens, expert_ids, gate_prob, w_gate, w_up, w_down):
    experts, tensors = lax.axis_size("expert"), lax.axis_size("tensor")
    me = lax.axis_index("expert")
    nx = ny = experts // 2
    nz = tensors // nx
    rows, columns = tokens.shape
    swap = [(e, e ^ 1) for e in range(experts)]
    core = lax.rem(me, 2)

    aux = jnp.concatenate(
        [expert_ids.astype(jnp.float32).T, gate_prob.T, jnp.zeros((4, rows), jnp.float32)], axis=0
    )
    blocks, table = gather(tokens, aux, nx, ny, nz)
    ids, prob = table[:, 0:2], table[:, 2:4]
    weight = jnp.sum(jnp.where(ids == me.astype(jnp.float32), prob, 0.0), axis=1)
    weight = weight.reshape(ny, 2, rows)

    def of_core(c):
        return lax.dynamic_index_in_dim(weight, c, 1, keepdims=False).reshape(ny * rows)

    mine = blocks.reshape(ny, tensors, rows, columns)
    mine = mine.transpose(0, 2, 1, 3).reshape(ny * rows, tensors * columns)
    theirs = lax.ppermute(mine, "expert", swap)

    def ffn(x, scale):
        gate = jnp.dot(x, w_gate[0], preferred_element_type=jnp.float32)
        up = jnp.dot(x, w_up[0], preferred_element_type=jnp.float32)
        hidden = (jax.nn.silu(gate) * up).astype(jnp.bfloat16)
        out = jnp.dot(hidden, w_down[0], preferred_element_type=jnp.float32)
        return out * scale[:, None]

    part_theirs = ffn(theirs, of_core(1 - core)).astype(jnp.bfloat16)
    arrived = lax.ppermute(part_theirs, "expert", swap)
    part_mine = ffn(mine, of_core(core))
    total = (part_mine + arrived.astype(jnp.float32)).astype(jnp.bfloat16)
    parts = total.reshape(ny, rows, tensors, columns).transpose(0, 2, 1, 3)
    return reduce_parts(parts.reshape(ny, nz, nx, rows, columns), nx, ny, nz)


def solution(mesh):
    return jax.shard_map(
        local,
        mesh=mesh,
        in_specs=(
            P("expert", "tensor"),
            P("expert", None),
            P("expert", None),
            P("expert", None, "tensor"),
            P("expert", None, "tensor"),
            P("expert", "tensor", None),
        ),
        out_specs=P("expert", "tensor"),
        check_vma=False,
    )
```

```python
import functools

import jax
import jax.numpy as jnp
from jax import lax
from jax.experimental import pallas as pl
from jax.experimental.pallas import tpu as pltpu
from jax.sharding import PartitionSpec as P

MESH = pl.DeviceIdType.MESH
VMEM_LIMIT = 56 * 1024 * 1024


def place(nx, nz):
    e, t = lax.axis_index("expert"), lax.axis_index("tensor")
    y, core = e // 2, lax.rem(e, 2)
    z, x = t // nx, lax.rem(t, nx)
    return e, x, y, z, core


def greet(lines):
    barrier = pltpu.get_barrier_semaphore()
    for device in lines:
        pl.semaphore_signal(barrier, inc=1, device_id=device, device_id_type=MESH)
    pl.semaphore_wait(barrier, len(lines))


def remote(src, dst, sems, device):
    send, recv = sems
    return pltpu.make_async_remote_copy(
        src_ref=src,
        dst_ref=dst,
        send_sem=send,
        recv_sem=recv,
        device_id=device,
        device_id_type=MESH,
    )


def is_flat(columns):
    return columns % 128 == 0


def slab(nx, columns, y, z, x, rows):
    if not is_flat(columns):
        return (y, z, x, rows)
    if isinstance(x, slice):
        start, width = z * (nx * columns), nx * columns
    else:
        start, width = (z * nx + x) * columns, columns
    return (y, rows, pl.ds(pl.multiple_of(start, columns), width))


def gathered(nx, ny, nz, rows, columns):
    if is_flat(columns):
        return (ny, rows, nz * nx * columns)
    return (ny, nz, nx, rows, columns)


def gather_kernel(
    nx, ny, nz, own_ref, aux_ref, g_ref, all_ref, s1, r1, s2, r2, s3, r3, s4, r4, sa, ra, local_sem
):
    e, x, y, z, core = place(nx, nz)
    experts = 2 * ny
    half = own_ref.shape[0] // 2
    t = z * nx + x
    partner = (2 * y + 1 - core, t)
    every = slice(None)

    def at(side, ys, zs, xs, r):
        return g_ref.at[(side, *slab(nx, own_ref.shape[1], ys, zs, xs, r))]

    def at_z(d):
        return (e, lax.rem(z + d, nz) * nx + x)

    def at_x(j):
        return (e, z * nx + lax.rem(x + j, nx))

    def at_y(j):
        return (lax.rem(y + j, ny) * 2 + core, t)

    def at_e(j):
        return (lax.rem(e + j, experts), t)

    greet(
        [at_z(d) for d in range(1, nz)]
        + [at_x(j) for j in range(1, nx)]
        + [at_e(j) for j in range(1, experts)]
    )
    waits = []
    rows = [pl.ds(0, half), pl.ds(half, half)]
    for h in range(2):
        keep = pltpu.make_async_copy(
            own_ref.at[rows[h]], at(0, y, z, x, rows[h]), local_sem.at[h]
        )
        keep.start()
        waits.append((keep, False))
    first = {}
    for d in range(1, nz):
        for h in range(2):
            c = remote(
                own_ref.at[rows[h]],
                at(0, y, z, x, rows[h]),
                (s1.at[h, d], r1.at[h, d]),
                at_z(d),
            )
            c.start()
            first[h, d] = c
    aux = []
    keep = pltpu.make_async_copy(aux_ref, all_ref.at[e], local_sem.at[2])
    keep.start()
    waits.append((keep, False))
    for j in range(1, experts):
        c = remote(aux_ref, all_ref.at[e], (sa.at[j], ra.at[j]), at_e(j))
        c.start()
        aux.append(c)

    second, third, fourth = {}, {}, {}

    def forward(d):
        zs = lax.rem(z + nz - d, nz)
        for h in range(2):
            if d:
                first[h, d].wait_recv()
                src = at(0, y, zs, x, rows[h])
            else:
                src = own_ref.at[rows[h]]
            n, to = ((nx, at_x), (ny, at_y))[h]
            for j in range(1, n):
                c = remote(
                    src, at(0, y, zs, x, rows[h]), (s2.at[h, d, j], r2.at[h, d, j]), to(j)
                )
                c.start()
                second[h, d, j] = c

    def spread(d):
        zs = lax.rem(z + nz - d, nz)
        for h in range(2):
            n, m, to = ((nx, ny, at_y), (ny, nx, at_x))[h]
            for j in range(1, n):
                second[h, d, j].wait_recv()
            if d == 0:
                waits[h][0].wait()
            line = (y, zs, every) if h == 0 else (every, zs, x)
            held = at(0, *line, rows[h])
            for k in range(1, m):
                c = remote(held, held, (s3.at[h, d, k], r3.at[h, d, k]), to(k))
                c.start()
                third[h, d, k] = c
            hand_over(h, d, 0, line)

    def hand_over(h, d, k, line):
        if not is_flat(own_ref.shape[1]):
            return
        c = remote(
            at(0, *line, rows[h]), at(1, *line, rows[h]), (s4.at[h, d, k], r4.at[h, d, k]), partner
        )
        c.start()
        fourth[h, d, k] = c

    def relay(d):
        zs = lax.rem(z + nz - d, nz)
        for k in range(1, max(nx, ny)):
            for h in range(2):
                if (h, d, k) in third:
                    third[h, d, k].wait_recv()
                    if h == 0:
                        line = (lax.rem(y + ny - k, ny), zs, every)
                    else:
                        line = (every, zs, lax.rem(x + nx - k, nx))
                    hand_over(h, d, k, line)

    forward(0)
    for d in range(1, nz):
        forward(d)
        spread(d - 1)
        if d > 1:
            relay(d - 2)
    spread(nz - 1)
    for d in range(max(nz - 2, 0), nz):
        relay(d)
    for c in fourth.values():
        c.wait_recv()
    for c in aux:
        c.wait()
    waits[2][0].wait()
    for c in [*first.values(), *second.values(), *third.values(), *fourth.values()]:
        c.wait_send()


def gather(tokens, aux, nx, ny, nz):
    rows, columns = tokens.shape
    n = max(nx, ny)
    dma = pltpu.SemaphoreType.DMA
    size = tokens.size * 2 * nx * ny * nz
    return pl.pallas_call(
        functools.partial(gather_kernel, nx, ny, nz),
        out_shape=(
            jax.ShapeDtypeStruct((1 + is_flat(columns), *gathered(nx, ny, nz, rows, columns)), tokens.dtype),
            jax.ShapeDtypeStruct((2 * ny, *aux.shape), aux.dtype),
        ),
        in_specs=[pl.BlockSpec(memory_space=pl.ANY)] * 2,
        out_specs=[pl.BlockSpec(memory_space=pl.ANY)] * 2,
        scratch_shapes=[
            dma((2, nz)),
            dma((2, nz)),
            dma((2, nz, n)),
            dma((2, nz, n)),
            dma((2, nz, n)),
            dma((2, nz, n)),
            dma((2, nz, n)),
            dma((2, nz, n)),
            dma((2 * ny,)),
            dma((2 * ny,)),
            dma((3,)),
        ],
        cost_estimate=pl.CostEstimate(flops=0, bytes_accessed=2 * size, transcendentals=0),
        compiler_params=pltpu.CompilerParams(collective_id=0, has_side_effects=True),
    )(tokens, aux)


def reduce_kernel(
    nx, ny, nz, p_ref, o_ref, ya, xa, yb, xb, yc, xc, za, zb, s1, r1, s2, r2, s3, r3
):
    e, x, y, z, core = place(nx, nz)
    half, columns = o_ref.shape[0] // 2, o_ref.shape[1]
    t = z * nx + x
    f32 = jnp.float32
    every = slice(None)

    def part(ys, zs, xs, r):
        return slab(nx, columns, ys, zs, xs, r)

    def entry(h, lead, i):
        if h == 0 and is_flat(columns):
            return (*lead, every, pl.ds(pl.multiple_of(i * columns, columns), columns))
        return (*lead, i)

    def at_z(d):
        return (e, lax.rem(z + d, nz) * nx + x)

    def at_x(j):
        return (e, z * nx + lax.rem(x + j, nx))

    def at_y(j):
        return (lax.rem(y + j, ny) * 2 + core, t)

    greet(
        [at_z(d) for d in range(1, nz)]
        + [at_x(j) for j in range(1, nx)]
        + [at_y(j) for j in range(1, ny)]
    )
    rows = [pl.ds(0, half), pl.ds(half, half)]
    order = [*range(1, nz), 0]
    one, two, three = {}, {}, {}
    got, held, last = (ya, xa), (yb, xb), (yc, xc)
    for d in order:
        zt = lax.rem(z + d, nz)
        for h in range(2):
            n, to = ((ny, at_y), (nx, at_x))[h]
            for j in range(1, n):
                if h == 0:
                    src = p_ref.at[part(lax.rem(y + j, ny), zt, every, rows[h])]
                else:
                    src = p_ref.at[part(every, zt, lax.rem(x + j, nx), rows[h])]
                c = remote(src, got[h].at[d, j - 1], (s1.at[h, d, j], r1.at[h, d, j]), to(j))
                c.start()
                one[h, d, j] = c

    def middle(d):
        zt = lax.rem(z + d, nz)
        for h in range(2):
            n, m, to, at = ((ny, nx, at_x, x), (nx, ny, at_y, y))[h]
            for j in range(1, n):
                one[h, d, j].wait_recv()

            def add(i, _, h=h, n=n):
                if h == 0:
                    total = p_ref[part(y, zt, i, rows[h])].astype(f32)
                else:
                    total = p_ref[part(i, zt, x, rows[h])].astype(f32)
                for j in range(n - 1):
                    total += got[h][entry(h, (d, j), i)].astype(f32)
                held[h][entry(h, (d,), i)] = total.astype(held[h].dtype)
                return 0

            lax.fori_loop(0, m, add, 0)
            for k in range(1, m):
                c = remote(
                    held[h].at[entry(h, (d,), lax.rem(at + k, m))],
                    last[h].at[d, k - 1],
                    (s2.at[h, d, k], r2.at[h, d, k]),
                    to(k),
                )
                c.start()
                two[h, d, k] = c

    def end(d):
        for h in range(2):
            m, at = ((nx, x), (ny, y))[h]
            for k in range(1, m):
                two[h, d, k].wait_recv()
            total = held[h][entry(h, (d,), at)].astype(f32)
            for k in range(m - 1):
                total += last[h][d, k].astype(f32)
            za[h, d] = total.astype(za.dtype)
            if d:
                c = remote(za.at[h, d], zb.at[h, d - 1], (s3.at[h, d], r3.at[h, d]), at_z(d))
                c.start()
                three[h, d] = c

    for i, d in enumerate(order):
        middle(d)
        if i:
            end(order[i - 1])
    end(order[-1])
    for h in range(2):
        total = za[h, 0].astype(f32)
        for d in range(1, nz):
            three[h, d].wait_recv()
            total += zb[h, d - 1].astype(f32)
        o_ref[rows[h], :] = total.astype(o_ref.dtype)
    for c in [*one.values(), *two.values(), *three.values()]:
        c.wait_send()


def reduce_parts(parts, rows, columns, nx, ny, nz):
    half, n = rows // 2, max(nx, ny)
    kind = parts.dtype
    dma = pltpu.SemaphoreType.DMA
    line = (half, nx * columns) if is_flat(columns) else (nx, half, columns)
    return pl.pallas_call(
        functools.partial(reduce_kernel, nx, ny, nz),
        out_shape=jax.ShapeDtypeStruct((rows, columns), kind),
        in_specs=[pl.BlockSpec(memory_space=pltpu.VMEM)],
        out_specs=pl.BlockSpec(memory_space=pltpu.VMEM),
        scratch_shapes=[
            pltpu.VMEM((nz, ny - 1, *line), kind),
            pltpu.VMEM((nz, nx - 1, ny, half, columns), kind),
            pltpu.VMEM((nz, *line), kind),
            pltpu.VMEM((nz, ny, half, columns), kind),
            pltpu.VMEM((nz, nx - 1, half, columns), kind),
            pltpu.VMEM((nz, ny - 1, half, columns), kind),
            pltpu.VMEM((2, nz, half, columns), kind),
            pltpu.VMEM((2, nz - 1, half, columns), kind),
            dma((2, nz, n)),
            dma((2, nz, n)),
            dma((2, nz, n)),
            dma((2, nz, n)),
            dma((2, nz)),
            dma((2, nz)),
        ],
        cost_estimate=pl.CostEstimate(flops=0, bytes_accessed=4 * parts.size, transcendentals=0),
        compiler_params=pltpu.CompilerParams(
            collective_id=1, has_side_effects=True, vmem_limit_bytes=VMEM_LIMIT
        ),
    )(parts)


def local(tokens, expert_ids, gate_prob, w_gate, w_up, w_down):
    experts, tensors = lax.axis_size("expert"), lax.axis_size("tensor")
    me = lax.axis_index("expert")
    nx = ny = experts // 2
    nz = tensors // nx
    rows, columns = tokens.shape
    swap = [(e, e ^ 1) for e in range(experts)]
    core = lax.rem(me, 2)

    aux = jnp.concatenate(
        [expert_ids.astype(jnp.float32).T, gate_prob.T, jnp.zeros((4, rows), jnp.float32)], axis=0
    )
    blocks, table = gather(tokens, aux, nx, ny, nz)
    ids, prob = table[:, 0:2], table[:, 2:4]
    weight = jnp.sum(jnp.where(ids == me.astype(jnp.float32), prob, 0.0), axis=1)
    weight = weight.reshape(ny, 2, rows)

    def of_core(c):
        return lax.dynamic_index_in_dim(weight, c, 1, keepdims=False).reshape(ny * rows)

    def up_half(x):
        gate = jnp.dot(x, w_gate[0], preferred_element_type=jnp.float32)
        up = jnp.dot(x, w_up[0], preferred_element_type=jnp.float32)
        return (jax.nn.silu(gate) * up).astype(jnp.bfloat16)

    if is_flat(columns):
        hidden = up_half(blocks.reshape(2 * ny * rows, tensors * columns))
        hidden_mine, hidden_theirs = hidden[: ny * rows], hidden[ny * rows :]
    else:
        mine = blocks.reshape(ny, tensors, rows, columns)
        mine = mine.transpose(0, 2, 1, 3).reshape(ny * rows, tensors * columns)
        theirs = lax.ppermute(mine, "expert", swap)
        hidden_mine, hidden_theirs = up_half(mine), up_half(theirs)

    def down(h, scale):
        return jnp.dot(h, w_down[0], preferred_element_type=jnp.float32) * scale[:, None]

    part_theirs = down(hidden_theirs, of_core(1 - core)).astype(jnp.bfloat16)
    arrived = lax.ppermute(part_theirs, "expert", swap)
    part_mine = down(hidden_mine, of_core(core))
    total = (part_mine + arrived.astype(jnp.float32)).astype(jnp.bfloat16)
    parts = total.reshape(ny, rows, tensors * columns)
    if not is_flat(columns):
        parts = parts.reshape(ny, rows, nz, nx, columns).transpose(0, 2, 3, 1, 4)
    return reduce_parts(parts, rows, columns, nx, ny, nz)


def solution(mesh):
    return jax.shard_map(
        local,
        mesh=mesh,
        in_specs=(
            P("expert", "tensor"),
            P("expert", None),
            P("expert", None),
            P("expert", None, "tensor"),
            P("expert", None, "tensor"),
            P("expert", "tensor", None),
        ),
        out_specs=P("expert", "tensor"),
        check_vma=False,
    )
```
